32 devices in a mesh: pairs: 2 (over y), src: 8 (over z, x), tgt: 2 (over core).
Axes of the slice: x: 2, y: 2, z: 4, core: 2. Of those that a mesh axis runs over, the one named last changes fastest.
Arguments:
- source_expr: bfloat16 [20480, 1024], P('src', 'pairs'), parts along dimension 1, may hold values from -6 to 6
- target_expr: bfloat16 [20480, 8192], P('src', 'pairs'), parts along dimension 1, may hold values from -6 to 6
- loadings: bfloat16 [20480, 50], P('src'), may hold values from -0.0390625 to 0.0390625
- panel: int32 [96], replicated, may hold values from 0 to 20479
- time_label: int32 [1024], P(('pairs', 'src')), parts along dimension 0, may hold values from 0 to 3
- target_order: int32 [8192], P('pairs'), parts along dimension 0, may hold values from 0 to 4095, each once
Outputs:
- coupling: float32 [1024, 4096], P(('pairs', 'src'), 'tgt'), parts along dimension 0
The draws below stay inside these ranges and needn't reach their ends.
There are 2 independent parts, one for each index of `pairs`. The reference program is written for one: setup_inputs(seed, part) draws one part's arguments, and reference() takes and returns one part's arrays. A program takes and returns all parts, laid end to end along the dimension named above; an argument that names none is the same for every part. Nothing has to cross between parts.
Inputs may be any that keep to these rules, and one draw needn't show every extreme that they name: `panel`: each entry is the index of a gene. `target_order`: a permutation of the target cells.
All inputs are finite; a program needn't handle non-finite values.
Results may differ from the reference program's by a relative error of at most 0.0003.
Values sent between devices are 32-bit elements; how exact they have to be, the bound alone decides.
A program may use at most 128 MiB of HBM per device.

```python
import jax
import jax.numpy as jnp
from jax import lax

G = 20480
K = 50
PANEL = 96
LEVELS = 4
ITERS = 3
NS = 512
NT = 4096


def set_ends(values, stream_key, low, top_value):
    place = [jax.random.randint(jax.random.fold_in(stream_key, axis), (), 0, length) for axis, length in enumerate(values.shape)]
    main_axis = values.shape.index(max(values.shape))
    beside = place[:main_axis] + [(place[main_axis] + 1) % values.shape[main_axis]] + place[main_axis + 1:]
    return values.at[tuple(place)].set(low).at[tuple(beside)].set(top_value)


def raised(drawn, rng, source, target, parts, factor):
    owner, partner = [(jnp.arange(drawn.shape[axis_at]) // (drawn.shape[axis_at] // parts)).reshape([-1 if axis == axis_at else 1 for axis in range(drawn.ndim)]) for axis_at in (source, target)]
    chosen = jax.random.permutation(rng, parts)[partner]
    strong = (owner == chosen) | (owner == (partner + parts // 2) % parts)
    return jnp.where(strong, factor * drawn, drawn)


def level_of(rng, dims, pieces, least, largest):
    level, own = 1.0, jax.random.fold_in(rng, 6)
    for position, blocks in pieces:
        heights = jnp.exp(jax.random.uniform(jax.random.fold_in(own, position), (blocks,), jnp.float32, least / len(pieces), largest / len(pieces)))
        level = level * jnp.repeat(heights, dims[position] // blocks).reshape([-1 if axis == position else 1 for axis in range(len(dims))])
    return level


def normal_values(rng, shape, deviation, reach, cuts=(), held_as=jnp.bfloat16):
    array = deviation * jax.random.normal(rng, shape, jnp.float32)
    if cuts:
        array = array * level_of(rng, shape, cuts, -0.22, 0.18)
    return jnp.clip(array, -reach, reach).astype(held_as)


def bell_draw_with(stream_key, shape, spread, reach, split, heavy, kind=jnp.bfloat16):
    values = spread * jax.random.normal(stream_key, shape, jnp.float32)
    if split:
        values = values * level_of(stream_key, shape, split, -0.22, 0.18)
    return jnp.clip(raised(values, jax.random.fold_in(stream_key, 3), *heavy), -reach, reach).astype(kind)


def setup_inputs(seed: int = 0, part: int = 0) -> dict:
    seeds = jax.random.split(jax.random.key(seed), 7)
    own_keys = jax.random.split(jax.random.fold_in(seeds[6], part), 7)
    return {
        "source_expr": bell_draw_with(own_keys[0], (G, NS), 1.0, 6.0, ((0, 8),), (0, 1, 8, 2.0)),
        "target_expr": normal_values(own_keys[1], (G, NT), 1.0, 6.0, ((0, 8),)),
        "loadings": normal_values(seeds[2], (G, K), G ** -0.5, 0.0390625, ((0, 8),)),
        "panel": set_ends(jax.random.randint(seeds[3], (PANEL,), 0, G), jax.random.fold_in(seeds[3], 1), 0, G - 1).astype(jnp.int32),
        "time_label": set_ends(jax.random.randint(own_keys[4], (NS,), 0, LEVELS), jax.random.fold_in(own_keys[4], 1), 0, LEVELS - 1).astype(jnp.int32),
        "target_order": jax.random.permutation(own_keys[5], NT).astype(jnp.int32),
    }


def reference(source_expr, target_expr, loadings, panel, time_label, target_order):
    gene_ids = jnp.arange(G, dtype=jnp.int32)
    counts = lax.optimization_barrier(jnp.sum((panel[:, None] == gene_ids[None, :]).astype(jnp.float32), axis=0)).astype(jnp.bfloat16)
    source_pc = lax.dot_general(loadings, source_expr, (((0,), (0,)), ((), ())), preferred_element_type=jnp.float32)
    score = jnp.dot(counts[None, :], source_expr, preferred_element_type=jnp.float32)[0] / jnp.sqrt(jnp.float32(PANEL))
    target_all = lax.dot_general(loadings, target_expr, (((0,), (0,)), ((), ())), preferred_element_type=jnp.float32)
    target_pc = jnp.take(target_all, target_order, axis=1)
    spans = 0.5 * (jnp.float32(LEVELS) - time_label.astype(jnp.float32))
    growth = jnp.exp(spans * jnp.clip(score, -2.0, 2.0))
    src_sq = lax.optimization_barrier(jnp.sum(source_pc * source_pc, axis=0))
    tgt_sq = lax.optimization_barrier(jnp.sum(target_pc * target_pc, axis=0))
    src_mean = lax.optimization_barrier(jnp.sum(source_pc, axis=1)) / jnp.float32(NS)
    tgt_mean = lax.optimization_barrier(jnp.sum(target_pc, axis=1)) / jnp.float32(NT)
    mean_d2 = jnp.sum(src_sq) / jnp.float32(NS) + jnp.sum(tgt_sq) / jnp.float32(NT) - 2.0 * jnp.sum(src_mean * tgt_mean)
    cross = lax.dot_general(source_pc, target_pc, (((0,), (0,)), ((), ())), precision=lax.Precision.HIGHEST)
    d2 = src_sq[:, None] + tgt_sq[None, :] - 2.0 * cross
    cost = d2 / mean_d2
    kernel = jnp.exp(-cost / 0.1)
    target_mass = jnp.float32(NS) / jnp.float32(NT)
    power = 1.0 / 1.1
    scale_v = jnp.ones((NT,), jnp.float32)
    scale_u = jnp.ones((NS,), jnp.float32)
    for step in range(ITERS):
        scale_u = (growth / jnp.dot(kernel, scale_v, precision=lax.Precision.HIGHEST)) ** power
        scale_v = (target_mass / jnp.dot(scale_u, kernel, precision=lax.Precision.HIGHEST)) ** power
    return jnp.float32(NT) * scale_u[:, None] * kernel * scale_v[None, :]
```

```python
import functools

import jax
import jax.numpy as jnp
from jax import lax
from jax.experimental import pallas as pl
from jax.experimental.pallas import tpu as pltpu
from jax.sharding import PartitionSpec as P

LEVELS = 4
ITERS = 3


def gene_sum(left, right):
    return lax.dot_general(
        left, right, (((0,), (0,)), ((), ())), preferred_element_type=jnp.float32
    )


def build_kernel(source_pc, target_pc, mean_d2):
    src_sq = jnp.sum(source_pc * source_pc, axis=0)
    tgt_sq = jnp.sum(target_pc * target_pc, axis=0)
    cross = lax.dot_general(
        source_pc, target_pc, (((0,), (0,)), ((), ())), precision=lax.Precision.HIGHEST
    )
    d2 = src_sq[:, None] + tgt_sq[None, :] - 2.0 * cross
    return jnp.exp(-(d2 / mean_d2) / 0.1)


def local(source_expr, target_expr, loadings, panel, time_label, target_order):
    genes = source_expr.shape[0]
    first_gene = lax.axis_index("src") * genes
    gene_ids = first_gene + lax.broadcasted_iota(jnp.int32, (genes, panel.shape[0]), 0)
    counts = jnp.sum((gene_ids == panel[None, :]).astype(jnp.float32), axis=1).astype(jnp.bfloat16)
    source_pc = lax.psum_scatter(
        gene_sum(loadings, source_expr), "src", scatter_dimension=1, tiled=True
    )
    score_part = jnp.dot(counts[None, :], source_expr, preferred_element_type=jnp.float32)
    score_raw = lax.psum_scatter(score_part, "src", scatter_dimension=1, tiled=True)[0]
    score = score_raw / jnp.sqrt(jnp.float32(panel.shape[0]))
    total_targets = target_expr.shape[1]
    total_sources = source_expr.shape[1]
    columns = total_targets // lax.axis_size("tgt")
    local_order = lax.dynamic_slice_in_dim(target_order, lax.axis_index("tgt") * columns, columns)
    target_all = lax.psum(gene_sum(loadings, target_expr), "src")
    target_pc = jnp.take(target_all, local_order, axis=1)
    src_share = 1.0 / jnp.float32(lax.axis_size("tgt"))
    tgt_share = 1.0 / jnp.float32(lax.axis_size("src"))
    src_sq_sum, src_vec, tgt_sq_sum, tgt_vec = lax.psum(
        (
            jnp.sum(source_pc * source_pc) * src_share,
            jnp.sum(source_pc, axis=1) * src_share,
            jnp.sum(target_pc * target_pc) * tgt_share,
            jnp.sum(target_pc, axis=1) * tgt_share,
        ),
        ("src", "tgt"),
    )
    src_mean = src_vec / jnp.float32(total_sources)
    tgt_mean = tgt_vec / jnp.float32(total_targets)
    mean_d2 = (
        src_sq_sum / jnp.float32(total_sources)
        + tgt_sq_sum / jnp.float32(total_targets)
        - 2.0 * jnp.sum(src_mean * tgt_mean)
    )
    spans = 0.5 * (jnp.float32(LEVELS) - time_label.astype(jnp.float32))
    growth = jnp.exp(spans * jnp.clip(score, -2.0, 2.0))
    target_mass = jnp.float32(total_sources) / jnp.float32(total_targets)
    power = 1.0 / 1.1
    stored = build_kernel(source_pc, target_pc, mean_d2)
    scale_v = jnp.ones((columns,), jnp.float32)
    scale_u = jnp.ones((source_pc.shape[1],), jnp.float32)
    for step in range(ITERS):
        row_part = jnp.dot(stored, scale_v, precision=lax.Precision.HIGHEST)
        scale_u = (growth / lax.psum(row_part, "tgt")) ** power
        col_part = jnp.dot(scale_u, stored, precision=lax.Precision.HIGHEST)
        scale_v = (target_mass / lax.psum(col_part, "src")) ** power
    return jnp.float32(total_targets) * scale_u[:, None] * stored * scale_v[None, :]

def proj(left, right):
    return lax.dot_general(left, right, (((1,), (0,)), ((), ())), preferred_element_type=jnp.float32)


def proj_nt(left, right, precision=None):
    return lax.dot_general(
        left, right, (((1,), (1,)), ((), ())), precision=precision, preferred_element_type=jnp.float32
    )


def exact(left, right):
    return lax.dot_general(
        left, right, (((1,), (0,)), ((), ())), precision=lax.Precision.HIGHEST, preferred_element_type=jnp.float32
    )


def power_of(x):
    return jnp.exp(jnp.log(x) * (1.0 / 1.1))


def iota(shape, axis):
    return lax.broadcasted_iota(jnp.int32, shape, axis)


def fused(
    n, components, source_hbm, target_hbm, load_ref, panel_ref, label_ref, order_ref, out_ref,
    xs, xt, weights, part_t, recv_t, part_s, recv_s, all_t, all_s, stat, rows, lookup, perm, cols,
    load_sem, rt_send, rt_recv, rs_send, rs_recv, as_send, as_recv, st_send, st_recv, at_send, at_recv,
    fw_send, fw_recv, it_send, it_recv, co_send, co_recv,
):
    me = lax.axis_index("src")
    core = lax.axis_index("tgt")
    slot = core * n + me
    genes = load_ref.shape[0]
    width = xt.shape[2]
    half_s = xs.shape[1]
    high = recv_t.shape[1]
    n_targets = target_hbm.shape[1]
    n_sources = source_hbm.shape[1]
    own = out_ref.shape[0]
    columns = out_ref.shape[1]
    deep = 8 * n

    def peer(d):
        return lax.rem(me + d, n)

    def remote(src, dst, send, recv, s, c):
        return pltpu.make_async_remote_copy(
            src_ref=src, dst_ref=dst, send_sem=send, recv_sem=recv,
            device_id={"src": s, "tgt": c}, device_id_type=pl.DeviceIdType.MESH,
        )

    others = [(d, e) for e in range(2) for d in range(n) if (d, e) != (0, 0)]

    turn = [n // 2 + k * sign for k in range(n // 2) for sign in ((1, -1) if k else (1,))] + [0]

    barrier = pltpu.get_barrier_semaphore()
    for d, e in others:
        pl.semaphore_signal(
            barrier, inc=1, device_id={"src": peer(d), "tgt": lax.rem(core + e, 2)},
            device_id_type=pl.DeviceIdType.MESH,
        )

    load_s = pltpu.make_async_copy(
        source_hbm.at[:, pl.ds(pl.multiple_of(core * half_s, 128), half_s)], xs, load_sem.at[n]
    )
    load_s.start()
    loads = []
    for d in turn:
        start = pl.multiple_of(core * columns + peer(d) * width, 128)
        load = pltpu.make_async_copy(target_hbm.at[:, pl.ds(start, width)], xt.at[d], load_sem.at[d])
        load.start()
        loads.append(load)

    eye = (iota((deep, components), 0) == iota((deep, components), 1)).astype(jnp.bfloat16)
    base = proj_nt(eye, load_ref[...])
    hits = (iota((genes, panel_ref.shape[1]), 0) + me * genes == panel_ref[...]).astype(jnp.float32)
    pick = (iota((deep, panel_ref.shape[1]), 0) == components).astype(jnp.bfloat16)
    counts = proj_nt(pick, hits.astype(jnp.bfloat16))
    weights[0] = base.astype(jnp.bfloat16)
    weights[1] = (base + counts).astype(jnp.bfloat16)

    spans = 0.5 * (LEVELS - label_ref[...].astype(jnp.float32))
    place = (iota((own, half_s), 0) + me * own == iota((own, half_s), 1) + core * half_s).astype(jnp.bfloat16)
    placed = proj(jnp.broadcast_to(spans, (16, own)).astype(jnp.bfloat16), place)[0:1]
    load_s.wait()
    source_part = proj(weights[1], xs[...])
    part_s[...] = jnp.where(iota((deep, half_s), 0) == components + 1, placed, source_part)
    recv_s[me] = part_s[pl.ds(pl.multiple_of(me * 8, 8), 8), :]

    pl.semaphore_wait(barrier, len(others))
    sends = []

    def go(copy):
        copy.start()
        sends.append(copy)

    for d in turn[:-1]:
        p = peer(d)
        go(remote(part_s.at[pl.ds(pl.multiple_of(p * 8, 8), 8)], recv_s.at[me], rs_send.at[d], rs_recv.at[me], p, core))

    for d, load in zip(turn, loads):
        load.wait()
        block = proj(weights[0], xt[d])[:high]
        if d:
            part_t[d] = block
            go(remote(part_t.at[d], recv_t.at[me], rt_send.at[d], rt_recv.at[me], peer(d), core))
        else:
            recv_t[me] = block

    for d in range(1, n):
        p = peer(d)
        remote(recv_s.at[p], recv_s.at[p], rs_send.at[d], rs_recv.at[p], p, core).wait_recv()
    my_rows = pl.ds(pl.multiple_of(me * 8, 8), 8)
    my_lanes = pl.ds(pl.multiple_of(core * half_s, 128), half_s)
    total = recv_s[0]
    for s in range(1, n):
        total = total + recv_s[s]
    all_s[my_rows, my_lanes] = total
    for q, (d, e) in enumerate(others):
        c = lax.rem(core + e, 2)
        here = all_s.at[my_rows, my_lanes]
        go(remote(here, here, as_send.at[q], as_recv.at[slot], peer(d), c))

    order = order_ref[:, pl.ds(pl.multiple_of(core * columns, 128), columns)]
    block_of = order // width
    lookup[...] = (iota((width, columns), 0) == order - block_of * width).astype(jnp.float32).astype(jnp.bfloat16)

    for d in range(1, n):
        p = peer(d)
        remote(recv_t.at[p], recv_t.at[p], rt_send.at[d], rt_recv.at[p], p, core).wait_recv()
    mine = recv_t[0]
    for s in range(1, n):
        mine = mine + recv_t[s]
    all_t[slot] = mine
    turned = jnp.transpose(jnp.concatenate([mine, jnp.zeros((128 - high, width), jnp.float32)], axis=0))
    sums = jnp.sum(turned, axis=0, keepdims=True)
    norms = jnp.sum(turned * turned, axis=1, keepdims=True)
    stat[slot] = jnp.where(iota((1, 128), 1) == 127, jnp.sum(norms, axis=0, keepdims=True), sums)
    for q, (d, e) in enumerate(others):
        c = lax.rem(core + e, 2)
        go(remote(stat.at[slot], stat.at[slot], st_send.at[q], st_recv.at[slot], peer(d), c))
    for d in turn:
        if d:
            go(remote(all_t.at[slot], all_t.at[slot], at_send.at[d], at_recv.at[me], peer(d), core))
    go(remote(all_t.at[slot], all_t.at[slot], fw_send.at[0], fw_recv.at[me], me, 1 - core))

    for q, (d, e) in enumerate(others):
        p, c = peer(d), lax.rem(core + e, 2)
        there = all_s.at[pl.ds(pl.multiple_of(p * 8, 8), 8), pl.ds(pl.multiple_of(c * half_s, 128), half_s)]
        remote(there, there, as_send.at[q], as_recv.at[c * n + p], p, c).wait_recv()
    source = all_s[...]
    growth = jnp.exp(
        source[components + 1 : components + 2]
        * jnp.clip(source[components : components + 1] / jnp.sqrt(jnp.float32(panel_ref.shape[1])), -2.0, 2.0)
    )
    pcs = jnp.where(iota(source.shape, 0) < components, source, 0.0)
    source_sq = jnp.sum(pcs * pcs, axis=0, keepdims=True)
    cross = exact(turned[:, :deep], pcs)
    d2 = norms + source_sq - 2.0 * cross
    mine_hot = (iota((own, n_sources), 0) + me * own == iota((own, n_sources), 1)).astype(jnp.float32)
    own_pc = proj_nt(mine_hot, pcs, lax.Precision.HIGHEST)
    own_sq = jnp.sum(own_pc * own_pc, axis=1, keepdims=True)

    for q, (d, e) in enumerate(others):
        p, c = peer(d), lax.rem(core + e, 2)
        there = stat.at[c * n + p]
        remote(there, there, st_send.at[q], st_recv.at[c * n + p], p, c).wait_recv()
    stats = stat[0]
    for s in range(1, 2 * n):
        stats = stats + stat[s]
    target_sq = jnp.sum(jnp.where(iota((1, 128), 1) == 127, stats, 0.0), axis=1, keepdims=True)
    dots = exact(jnp.broadcast_to(stats[:, :deep], (8, deep)), pcs)[0:1]
    mean = (
        jnp.sum(source_sq, axis=1, keepdims=True) / n_sources
        + target_sq / n_targets
        - 2.0 * (jnp.sum(dots, axis=1, keepdims=True) / n_sources / n_targets)
    )
    stored = jnp.exp(-(d2 / mean) / 0.1)

    def spread(step, values):
        rows[step, slot] = values
        for q, (d, e) in enumerate(others):
            c = lax.rem(core + e, 2)
            here = rows.at[step, slot]
            go(remote(here, here, it_send.at[step, q], it_recv.at[step, slot], peer(d), c))

    def gather(step):
        for q, (d, e) in enumerate(others):
            p, c = peer(d), lax.rem(core + e, 2)
            there = rows.at[step, c * n + p]
            remote(there, there, it_send.at[step, q], it_recv.at[step, c * n + p], p, c).wait_recv()
        full = rows[step, 0]
        for s in range(1, 2 * n):
            full = full + rows[step, s]
        return power_of(growth / full)

    def place_blocks(first):
        @pl.loop(0, n)
        def _(k):
            index = first + k
            block = all_t[index]
            top = block.astype(jnp.bfloat16).astype(jnp.float32)
            rest = block - top
            middle = rest.astype(jnp.bfloat16).astype(jnp.float32)
            three = jnp.concatenate([top, middle, rest - middle], axis=0).astype(jnp.bfloat16)
            found = proj(three, lookup[...])
            found = (found[:high] + found[high : 2 * high]) + found[2 * high :]
            perm[...] = jnp.where(block_of == index, found, perm[...])

    target_mass = n_sources / n_targets
    spread(0, jnp.sum(stored, axis=0, keepdims=True))
    perm[...] = jnp.zeros_like(perm)
    scale_u = gather(0)
    scale_v = power_of(target_mass / jnp.sum(stored * scale_u, axis=1, keepdims=True))
    spread(1, jnp.sum(stored * scale_v, axis=0, keepdims=True))
    for d in turn[:-1]:
        p = peer(d)
        there = all_t.at[core * n + p]
        remote(there, there, at_send.at[d], at_recv.at[p], p, core).wait_recv()
        go(remote(there, there, fw_send.at[d], fw_recv.at[p], me, 1 - core))
    place_blocks(core * n)
    scale_u = gather(1)
    scale_v = power_of(target_mass / jnp.sum(stored * scale_u, axis=1, keepdims=True))
    spread(2, jnp.sum(stored * scale_v, axis=0, keepdims=True))
    for d in range(n):
        p = peer(d)
        there = all_t.at[(1 - core) * n + p]
        remote(there, there, fw_send.at[d], fw_recv.at[p], me, 1 - core).wait_recv()
    place_blocks((1 - core) * n)
    placed_t = perm[...]
    placed_sq = jnp.sum(placed_t * placed_t, axis=0, keepdims=True)
    out_ref[...] = jnp.exp(-((own_sq + placed_sq - 2.0 * exact(own_pc[:, :high], placed_t)) / mean) / 0.1)
    scale_u = gather(2)
    own_u = jnp.sum(mine_hot * scale_u, axis=1, keepdims=True)
    cols[me] = jnp.sum(out_ref[...] * own_u, axis=0, keepdims=True)
    for d in range(1, n):
        go(remote(cols.at[me], cols.at[me], co_send.at[d], co_recv.at[me], peer(d), core))
    out_ref[...] = n_targets * own_u * out_ref[...]
    for d in range(1, n):
        p = peer(d)
        remote(cols.at[p], cols.at[p], co_send.at[d], co_recv.at[p], p, core).wait_recv()
    full = cols[0]
    for s in range(1, n):
        full = full + cols[s]
    out_ref[...] = out_ref[...] * power_of(target_mass / full)
    for copy in sends:
        copy.wait_send()


def fused_call(source_expr, target_expr, loadings, panel, time_label, target_order):
    n = lax.axis_size("src")
    genes, components = loadings.shape
    n_sources, n_targets = source_expr.shape[1], target_expr.shape[1]
    own, columns = n_sources // n, n_targets // 2
    width, half_s = columns // n, n_sources // 2
    high = (components + 7) // 8 * 8
    vmem = pl.BlockSpec(memory_space=pltpu.VMEM)
    any_spec = pl.BlockSpec(memory_space=pl.ANY)
    dma = pltpu.SemaphoreType.DMA
    f32 = jnp.float32
    return pl.pallas_call(
        functools.partial(fused, n, components),
        out_shape=jax.ShapeDtypeStruct((own, columns), f32),
        in_specs=[any_spec, any_spec, vmem, vmem, vmem, vmem],
        out_specs=vmem,
        scratch_shapes=[
            pltpu.VMEM((genes, half_s), jnp.bfloat16),
            pltpu.VMEM((n, genes, width), jnp.bfloat16),
            pltpu.VMEM((2, 8 * n, genes), jnp.bfloat16),
            pltpu.VMEM((n, high, width), f32),
            pltpu.VMEM((n, high, width), f32),
            pltpu.VMEM((8 * n, half_s), f32),
            pltpu.VMEM((n, 8, half_s), f32),
            pltpu.VMEM((2 * n, high, width), f32),
            pltpu.VMEM((8 * n, n_sources), f32),
            pltpu.VMEM((2 * n, 1, 128), f32),
            pltpu.VMEM((ITERS, 2 * n, 1, n_sources), f32),
            pltpu.VMEM((width, columns), jnp.bfloat16),
            pltpu.VMEM((high, columns), f32),
            pltpu.VMEM((n, 1, columns), f32),
            dma((n + 1,)),
            dma((n,)), dma((n,)), dma((n,)), dma((n,)),
            dma((2 * n,)), dma((2 * n,)), dma((2 * n,)), dma((2 * n,)),
            dma((n,)), dma((n,)), dma((n,)), dma((n,)),
            dma((ITERS, 2 * n)), dma((ITERS, 2 * n)),
            dma((n,)), dma((n,)),
        ],
        compiler_params=pltpu.CompilerParams(
            collective_id=0, has_side_effects=True, vmem_limit_bytes=48 * 1024 * 1024
        ),
    )(
        source_expr, target_expr, loadings,
        panel.reshape(1, -1), time_label.reshape(1, -1), target_order.reshape(1, -1),
    )


def fits(mesh, source_expr, target_expr, loadings, time_label):
    n = mesh.shape["src"]
    components = loadings.shape[1]
    n_sources, n_targets = source_expr.shape[1], target_expr.shape[1]
    return (
        mesh.shape["tgt"] == 2
        and n % 2 == 0
        and components + 2 <= 8 * n
        and 8 * n <= 126
        and n_sources % 256 == 0
        and n_targets % (2 * n * 128) == 0
        and loadings.shape[0] % 128 == 0
        and loadings.shape[0] * (n_targets + n_sources) <= 32 * 1024 * 1024
    )


def solution(mesh):
    def per_device(*arrays):
        if fits(mesh, arrays[0], arrays[1], arrays[2], arrays[4]):
            return fused_call(*arrays)
        return local(*arrays)

    return jax.shard_map(
        per_device,
        mesh=mesh,
        in_specs=(
            P("src", "pairs"),
            P("src", "pairs"),
            P("src", None),
            P(),
            P(("pairs", "src")),
            P("pairs"),
        ),
        out_specs=P(("pairs", "src"), "tgt"),
        check_vma=False,
    )
```

```python
import functools

import jax
import jax.numpy as jnp
from jax import lax
from jax.experimental import pallas as pl
from jax.experimental.pallas import tpu as pltpu
from jax.sharding import PartitionSpec as P

LEVELS = 4
ITERS = 3


def gene_sum(left, right):
    return lax.dot_general(
        left, right, (((0,), (0,)), ((), ())), preferred_element_type=jnp.float32
    )


def build_kernel(source_pc, target_pc, mean_d2):
    src_sq = jnp.sum(source_pc * source_pc, axis=0)
    tgt_sq = jnp.sum(target_pc * target_pc, axis=0)
    cross = lax.dot_general(
        source_pc, target_pc, (((0,), (0,)), ((), ())), precision=lax.Precision.HIGHEST
    )
    d2 = src_sq[:, None] + tgt_sq[None, :] - 2.0 * cross
    return jnp.exp(-(d2 / mean_d2) / 0.1)


def local(source_expr, target_expr, loadings, panel, time_label, target_order):
    genes = source_expr.shape[0]
    first_gene = lax.axis_index("src") * genes
    gene_ids = first_gene + lax.broadcasted_iota(jnp.int32, (genes, panel.shape[0]), 0)
    counts = jnp.sum((gene_ids == panel[None, :]).astype(jnp.float32), axis=1).astype(jnp.bfloat16)
    source_pc = lax.psum_scatter(
        gene_sum(loadings, source_expr), "src", scatter_dimension=1, tiled=True
    )
    score_part = jnp.dot(counts[None, :], source_expr, preferred_element_type=jnp.float32)
    score_raw = lax.psum_scatter(score_part, "src", scatter_dimension=1, tiled=True)[0]
    score = score_raw / jnp.sqrt(jnp.float32(panel.shape[0]))
    total_targets = target_expr.shape[1]
    total_sources = source_expr.shape[1]
    columns = total_targets // lax.axis_size("tgt")
    local_order = lax.dynamic_slice_in_dim(target_order, lax.axis_index("tgt") * columns, columns)
    target_all = lax.psum(gene_sum(loadings, target_expr), "src")
    target_pc = jnp.take(target_all, local_order, axis=1)
    src_share = 1.0 / jnp.float32(lax.axis_size("tgt"))
    tgt_share = 1.0 / jnp.float32(lax.axis_size("src"))
    src_sq_sum, src_vec, tgt_sq_sum, tgt_vec = lax.psum(
        (
            jnp.sum(source_pc * source_pc) * src_share,
            jnp.sum(source_pc, axis=1) * src_share,
            jnp.sum(target_pc * target_pc) * tgt_share,
            jnp.sum(target_pc, axis=1) * tgt_share,
        ),
        ("src", "tgt"),
    )
    src_mean = src_vec / jnp.float32(total_sources)
    tgt_mean = tgt_vec / jnp.float32(total_targets)
    mean_d2 = (
        src_sq_sum / jnp.float32(total_sources)
        + tgt_sq_sum / jnp.float32(total_targets)
        - 2.0 * jnp.sum(src_mean * tgt_mean)
    )
    spans = 0.5 * (jnp.float32(LEVELS) - time_label.astype(jnp.float32))
    growth = jnp.exp(spans * jnp.clip(score, -2.0, 2.0))
    target_mass = jnp.float32(total_sources) / jnp.float32(total_targets)
    power = 1.0 / 1.1
    stored = build_kernel(source_pc, target_pc, mean_d2)
    scale_v = jnp.ones((columns,), jnp.float32)
    scale_u = jnp.ones((source_pc.shape[1],), jnp.float32)
    for step in range(ITERS):
        row_part = jnp.dot(stored, scale_v, precision=lax.Precision.HIGHEST)
        scale_u = (growth / lax.psum(row_part, "tgt")) ** power
        col_part = jnp.dot(scale_u, stored, precision=lax.Precision.HIGHEST)
        scale_v = (target_mass / lax.psum(col_part, "src")) ** power
    return jnp.float32(total_targets) * scale_u[:, None] * stored * scale_v[None, :]

def proj(left, right):
    return lax.dot_general(left, right, (((1,), (0,)), ((), ())), preferred_element_type=jnp.float32)


def proj_nt(left, right, precision=None):
    return lax.dot_general(
        left, right, (((1,), (1,)), ((), ())), precision=precision, preferred_element_type=jnp.float32
    )


def power_of(x):
    return jnp.exp(jnp.log(x) * (1.0 / 1.1))


def iota(shape, axis):
    return lax.broadcasted_iota(jnp.int32, shape, axis)


def halves(x):
    top = x.astype(jnp.bfloat16).astype(jnp.float32)
    rest = x - top
    middle = rest.astype(jnp.bfloat16).astype(jnp.float32)
    return top, middle, rest - middle


def replicate(row):
    return jnp.transpose(jnp.broadcast_to(row, (128, row.shape[1])))


def fused(
    n, source_hbm, target_hbm, load_ref, panel_hbm, label_hbm, order_hbm, out_ref,
    panel_ref, label_ref, order_ref,
    xs, xt, weights, part_t, recv_x, sum_t, recv_t, part_s, recv_s, all_t, all_s, rows, lookup, perm, moments,
    kern, row_u, col_v,
    load_sem, small_sem, rx_send, rx_recv, rt_send, rt_recv, rs_send, rs_recv, as_send, as_recv, fs_send, fs_recv,
    ax_send, ax_recv, az_send, az_recv, fw_send, fw_recv, it_send, it_recv,
):
    me = lax.axis_index("src")
    core = lax.axis_index("tgt")
    nz = n // 2
    x = lax.rem(me, 2)
    z = me // 2
    beside = 2 * z + 1 - x
    components, genes = load_ref.shape
    width = xt.shape[2]
    half_s = xs.shape[1]
    high = part_t.shape[1]
    n_targets = target_hbm.shape[1]
    n_sources = source_hbm.shape[1]
    own = out_ref.shape[0]
    columns = out_ref.shape[1]
    deep = 8 * n

    def peer(d):
        return lax.rem(me + d, n)

    def along(d):
        return lax.rem(z + d, nz)

    def remote(src, dst, send, recv, s, c):
        return pltpu.make_async_remote_copy(
            src_ref=src, dst_ref=dst, send_sem=send, recv_sem=recv,
            device_id={"src": s, "tgt": c}, device_id_type=pl.DeviceIdType.MESH,
        )

    sends = []

    def go(copy):
        copy.start()
        sends.append(copy)

    turn = [n // 2 + k * sign for k in range(n // 2) for sign in ((1, -1) if k else (1,))]
    line = [nz // 2] + [d for d in range(1, nz) if d != nz // 2] + [0]

    barrier = pltpu.get_barrier_semaphore()
    for d in range(1, n):
        pl.semaphore_signal(
            barrier, inc=1, device_id={"src": peer(d), "tgt": core}, device_id_type=pl.DeviceIdType.MESH
        )
    pl.semaphore_signal(
        barrier, inc=1, device_id={"src": me, "tgt": 1 - core}, device_id_type=pl.DeviceIdType.MESH
    )

    small = []
    my_columns = pl.multiple_of(core * columns, 128)
    for k, (src, dst) in enumerate((
        (panel_hbm, panel_ref), (label_hbm, label_ref),
        (order_hbm.at[:, pl.ds(my_columns, columns)], order_ref),
    )):
        small.append(pltpu.make_async_copy(src, dst, small_sem.at[k]))
        small[-1].start()
    load_s = pltpu.make_async_copy(
        source_hbm.at[:, pl.ds(pl.multiple_of(core * half_s, 128), half_s)], xs, load_sem.at[n]
    )
    load_s.start()
    plan = [(d, 2 * along(d) + 1 - x) for d in line] + [(d, 2 * along(d) + x) for d in line]
    loads = []
    for k, (d, s) in enumerate(plan):
        start = pl.multiple_of(core * columns + s * width, 128)
        load = pltpu.make_async_copy(target_hbm.at[:, pl.ds(start, width)], xt.at[k], load_sem.at[k])
        load.start()
        loads.append(load)

    for copy in small:
        copy.wait()
    base = jnp.concatenate(
        [load_ref[...].astype(jnp.float32), jnp.zeros((deep - components, genes), jnp.float32)], axis=0
    )
    hits = (iota((genes, panel_ref.shape[1]), 0) + me * genes == panel_ref[...]).astype(jnp.float32)
    pick = (iota((deep, panel_ref.shape[1]), 0) == components).astype(jnp.bfloat16)
    counts = proj_nt(pick, hits.astype(jnp.bfloat16))
    weights[0] = base.astype(jnp.bfloat16)
    weights[1] = (base + counts).astype(jnp.bfloat16)

    spans = 0.5 * (LEVELS - label_ref[...].astype(jnp.float32))
    place = (iota((own, half_s), 0) + me * own == iota((own, half_s), 1) + core * half_s).astype(jnp.bfloat16)
    placed = proj(jnp.broadcast_to(spans, (16, own)).astype(jnp.bfloat16), place)[0:1]
    load_s.wait()
    source_part = proj(weights[1], xs[...])
    part_s[...] = jnp.where(iota((deep, half_s), 0) == components + 1, placed, source_part)
    recv_s[me] = part_s[pl.ds(pl.multiple_of(me * 8, 8), 8), :]

    pl.semaphore_wait(barrier, n)
    for d in turn:
        p = peer(d)
        go(remote(part_s.at[pl.ds(pl.multiple_of(p * 8, 8), 8)], recv_s.at[me], rs_send.at[d], rs_recv.at[me], p, core))

    for k, (d, s) in enumerate(plan):
        loads[k].wait()
        block = proj(weights[0], xt[k])[:high]
        zz = along(d)
        if k < nz:
            part_t[k] = block
            go(remote(part_t.at[k], recv_x.at[zz], rx_send.at[k], rx_recv.at[zz], beside, core))
        else:
            remote(recv_x.at[zz], recv_x.at[zz], rx_send.at[k - nz], rx_recv.at[zz], beside, core).wait_recv()
            block = block + recv_x[zz]
            if d:
                sum_t[d] = block
                go(remote(sum_t.at[d], recv_t.at[z], rt_send.at[d], rt_recv.at[z], s, core))
            else:
                recv_t[z] = block

    for d in turn:
        p = peer(d)
        remote(recv_s.at[p], recv_s.at[p], rs_send.at[d], rs_recv.at[p], p, core).wait_recv()
    my_lanes = pl.ds(pl.multiple_of(core * half_s, 128), half_s)
    other_lanes = pl.ds(pl.multiple_of((1 - core) * half_s, 128), half_s)

    def rows_of(s):
        return pl.ds(pl.multiple_of(s * 8, 8), 8)

    total = recv_s[0]
    for s in range(1, n):
        total = total + recv_s[s]
    all_s[rows_of(me), my_lanes] = total
    here = all_s.at[rows_of(me), my_lanes]
    for d in turn:
        go(remote(here, here, as_send.at[d], as_recv.at[me], peer(d), core))
    go(remote(here, here, fs_send.at[0], fs_recv.at[me], me, 1 - core))

    order = order_ref[...]
    block_of = order // width
    lookup[...] = (iota((width, columns), 0) == order - block_of * width).astype(jnp.float32).astype(jnp.bfloat16)
    perm[...] = jnp.zeros_like(perm)
    moments[...] = jnp.zeros_like(moments)

    def place_block(index):
        block = all_t[index]
        moments[0] += block
        moments[1] += block * block
        found = proj(jnp.concatenate(halves(block), axis=0).astype(jnp.bfloat16), lookup[...])
        found = (found[:high] + found[high : 2 * high]) + found[2 * high :]
        perm[:high] = jnp.where(block_of == index, found, perm[:high])

    for d in line[:-1]:
        zz = along(d)
        remote(recv_t.at[zz], recv_t.at[zz], rt_send.at[d], rt_recv.at[zz], 2 * zz + x, core).wait_recv()
    mine = recv_t[0]
    for s in range(1, nz):
        mine = mine + recv_t[s]
    slot = core * n + me
    all_t[slot] = mine
    here = all_t.at[slot]
    for d in line[:-1]:
        go(remote(here, here, az_send.at[d], az_recv.at[z], 2 * along(d) + x, core))
    go(remote(here, here, ax_send.at[0], ax_recv.at[z], beside, core))
    go(remote(here, here, fw_send.at[0, 0], fw_recv.at[me], me, 1 - core))

    for d in turn:
        p = peer(d)
        there = all_s.at[rows_of(p), my_lanes]
        remote(there, there, as_send.at[d], as_recv.at[p], p, core).wait_recv()
        go(remote(there, there, fs_send.at[d], fs_recv.at[p], me, 1 - core))
    place_block(slot)
    for d in line[:-1][::-1]:
        zz = along(d)
        s = 2 * zz + x
        there = all_t.at[core * n + s]
        remote(there, there, az_send.at[d], az_recv.at[zz], s, core).wait_recv()
        go(remote(there, there, ax_send.at[d], ax_recv.at[zz], beside, core))
        go(remote(there, there, fw_send.at[0, d], fw_recv.at[s], me, 1 - core))
        place_block(core * n + s)
    for d in line[::-1]:
        zz = along(d)
        s = 2 * zz + 1 - x
        there = all_t.at[core * n + s]
        remote(there, there, ax_send.at[d], ax_recv.at[zz], beside, core).wait_recv()
        go(remote(there, there, fw_send.at[1, d], fw_recv.at[s], me, 1 - core))
        place_block(core * n + s)

    for d in range(n):
        p = peer(d)
        there = all_s.at[rows_of(p), other_lanes]
        remote(there, there, fs_send.at[d], fs_recv.at[p], me, 1 - core).wait_recv()
    source = all_s[...]
    growth = jnp.exp(
        source[components + 1 : components + 2]
        * jnp.clip(source[components : components + 1] / jnp.sqrt(jnp.float32(panel_ref.shape[1])), -2.0, 2.0)
    )
    pcs = jnp.where(iota(source.shape, 0) < components, source, 0.0)
    source_sq = jnp.sum(pcs * pcs, axis=0, keepdims=True)
    source_rep = replicate(source_sq)
    turned = jnp.transpose(jnp.concatenate([pcs, jnp.zeros((128 - deep, n_sources), jnp.float32)], axis=0))
    s_top, s_mid, s_low = halves(turned[:, :deep])
    left = jnp.concatenate([s_top, s_mid, s_top, s_mid, s_low, s_top], axis=1).astype(jnp.bfloat16)

    for d in range(n):
        p = peer(d)
        there = all_t.at[(1 - core) * n + p]
        remote(there, there, fw_send.at[0, 0], fw_recv.at[p], me, 1 - core).wait_recv()

    @pl.loop(0, n)
    def _(k):
        place_block((1 - core) * n + k)

    target_sum = jnp.sum(moments[0], axis=1, keepdims=True)
    target_sq = jnp.sum(jnp.sum(moments[1], axis=1, keepdims=True), axis=0, keepdims=True)
    source_sum = jnp.sum(pcs[:high], axis=1, keepdims=True)
    mean = (
        jnp.sum(source_sq, axis=1, keepdims=True) / n_sources
        + target_sq / n_targets
        - 2.0 * jnp.sum((source_sum / n_sources) * (target_sum / n_targets), axis=0, keepdims=True)
    )
    factor = -1.0 / (0.1 * mean)
    tiles = columns // 128

    def lanes(t):
        return slice(t * 128, t * 128 + 128)

    step_rows = 64

    for t in range(0, tiles, 2):
        wide = slice(t * 128, t * 128 + 256)
        part = perm[:, wide]
        norm = jnp.sum(part * part, axis=0, keepdims=True)
        t_top, t_mid, t_low = halves(part)
        right = jnp.concatenate([t_top, t_top, t_mid, t_mid, t_top, t_low], axis=0).astype(jnp.bfloat16)
        cross = proj(left, right)
        for h in range(2):
            d2 = source_rep + norm[:, lanes(h)] - 2.0 * cross[:, lanes(h)]
            kern[:, lanes(t + h)] = jnp.exp(d2 * factor)

    def row_sums(scale):
        out = []
        for r in range(0, n_sources, step_rows):
            acc = None
            for t in range(tiles):
                term = kern[r : r + step_rows, lanes(t)]
                if scale:
                    term = term * col_v[:, lanes(t)]
                acc = term if acc is None else acc + term
            out.append(acc)
        return jnp.sum(jnp.transpose(jnp.concatenate(out, axis=0)), axis=0, keepdims=True)

    target_mass = n_sources / n_targets
    for step in range(ITERS):
        rows[step, core] = row_sums(step > 0)
        here = rows.at[step, core]
        go(remote(here, here, it_send.at[step], it_recv.at[step], me, 1 - core))
        there = rows.at[step, 1 - core]
        remote(there, there, it_send.at[step], it_recv.at[step], me, 1 - core).wait_recv()
        row_u[...] = replicate(power_of(growth / (rows[step, 0] + rows[step, 1])))
        for t in range(tiles):
            col_v[:, lanes(t)] = jnp.sum(kern[:, lanes(t)] * row_u[...], axis=0, keepdims=True)
        col_v[...] = power_of(target_mass / col_v[...])
    mine_rows = pl.ds(pl.multiple_of(me * own, 8), own)
    own_u = n_targets * row_u[mine_rows, :]
    for t in range(tiles):
        out_ref[:, lanes(t)] = own_u * kern[mine_rows, lanes(t)] * col_v[:, lanes(t)]
    for copy in sends:
        copy.wait_send()


def fused_call(source_expr, target_expr, loadings, panel, time_label, target_order):
    n = lax.axis_size("src")
    genes, components = loadings.shape
    n_sources, n_targets = source_expr.shape[1], target_expr.shape[1]
    own, columns = n_sources // n, n_targets // 2
    width, half_s = columns // n, n_sources // 2
    high = (components + 7) // 8 * 8
    nz = n // 2
    vmem = pltpu.VMEM
    dma = pltpu.SemaphoreType.DMA
    f32, bf16, i32 = jnp.float32, jnp.bfloat16, jnp.int32
    return pl.pallas_call(
        functools.partial(fused, n),
        out_shape=jax.ShapeDtypeStruct((own, columns), f32),
        in_specs=[pl.BlockSpec(memory_space=vmem if k == 2 else pltpu.HBM) for k in range(6)],
        out_specs=pl.BlockSpec(memory_space=vmem),
        scratch_shapes=[
            vmem((1, panel.shape[0]), i32),
            vmem((1, own), i32),
            vmem((1, columns), i32),
            vmem((genes, half_s), bf16),
            vmem((n, genes, width), bf16),
            vmem((2, 8 * n, genes), bf16),
            vmem((nz, high, width), f32),
            vmem((nz, high, width), f32),
            vmem((nz, high, width), f32),
            vmem((nz, high, width), f32),
            vmem((8 * n, half_s), f32),
            vmem((n, 8, half_s), f32),
            vmem((2 * n, high, width), f32),
            vmem((8 * n, n_sources), f32),
            vmem((ITERS, 2, 1, n_sources), f32),
            vmem((width, columns), bf16),
            vmem((8 * n, columns), f32),
            vmem((2, high, width), f32),
            vmem((n_sources, columns), f32),
            vmem((n_sources, 128), f32),
            vmem((1, columns), f32),
            dma((n + 1,)), dma((3,)),
            dma((nz,)), dma((nz,)), dma((nz,)), dma((nz,)),
            dma((n,)), dma((n,)), dma((n,)), dma((n,)), dma((n,)), dma((n,)),
            dma((nz,)), dma((nz,)), dma((nz,)), dma((nz,)),
            dma((2, nz)), dma((n,)), dma((ITERS,)), dma((ITERS,)),
        ],
        compiler_params=pltpu.CompilerParams(
            collective_id=0, has_side_effects=True, vmem_limit_bytes=48 * 1024 * 1024
        ),
    )(
        source_expr, target_expr, loadings.T,
        panel.reshape(1, -1), time_label.reshape(1, -1), target_order.reshape(1, -1),
    )


def fits(mesh, source_expr, target_expr, loadings, time_label):
    n = mesh.shape["src"]
    components = loadings.shape[1]
    n_sources, n_targets = source_expr.shape[1], target_expr.shape[1]
    return (
        mesh.shape["tgt"] == 2
        and n % 2 == 0
        and components + 2 <= 8 * n
        and 8 * n <= 128
        and n_sources % 256 == 0
        and n_sources * n_targets <= 2 * 1024 * 1024
        and n_targets % (2 * n * 128) == 0
        and loadings.shape[0] % 128 == 0
        and loadings.shape[0] * (n_targets + n_sources) <= 32 * 1024 * 1024
    )


def solution(mesh):
    def per_device(*arrays):
        if fits(mesh, arrays[0], arrays[1], arrays[2], arrays[4]):
            return fused_call(*arrays)
        return local(*arrays)

    return jax.shard_map(
        per_device,
        mesh=mesh,
        in_specs=(
            P("src", "pairs"),
            P("src", "pairs"),
            P("src", None),
            P(),
            P(("pairs", "src")),
            P("pairs"),
        ),
        out_specs=P(("pairs", "src"), "tgt"),
        check_vma=False,
    )
```

```python
import functools

import jax
import jax.numpy as jnp
from jax import lax
from jax.experimental import pallas as pl
from jax.experimental.pallas import tpu as pltpu
from jax.sharding import PartitionSpec as P

LEVELS = 4
ITERS = 3


def gene_sum(left, right):
    return lax.dot_general(
        left, right, (((0,), (0,)), ((), ())), preferred_element_type=jnp.float32
    )


def build_kernel(source_pc, target_pc, mean_d2):
    src_sq = jnp.sum(source_pc * source_pc, axis=0)
    tgt_sq = jnp.sum(target_pc * target_pc, axis=0)
    cross = lax.dot_general(
        source_pc, target_pc, (((0,), (0,)), ((), ())), precision=lax.Precision.HIGHEST
    )
    d2 = src_sq[:, None] + tgt_sq[None, :] - 2.0 * cross
    return jnp.exp(-(d2 / mean_d2) / 0.1)


def local(source_expr, target_expr, loadings, panel, time_label, target_order):
    genes = source_expr.shape[0]
    first_gene = lax.axis_index("src") * genes
    gene_ids = first_gene + lax.broadcasted_iota(jnp.int32, (genes, panel.shape[0]), 0)
    counts = jnp.sum((gene_ids == panel[None, :]).astype(jnp.float32), axis=1).astype(jnp.bfloat16)
    source_pc = lax.psum_scatter(
        gene_sum(loadings, source_expr), "src", scatter_dimension=1, tiled=True
    )
    score_part = jnp.dot(counts[None, :], source_expr, preferred_element_type=jnp.float32)
    score_raw = lax.psum_scatter(score_part, "src", scatter_dimension=1, tiled=True)[0]
    score = score_raw / jnp.sqrt(jnp.float32(panel.shape[0]))
    total_targets = target_expr.shape[1]
    total_sources = source_expr.shape[1]
    columns = total_targets // lax.axis_size("tgt")
    local_order = lax.dynamic_slice_in_dim(target_order, lax.axis_index("tgt") * columns, columns)
    target_all = lax.psum(gene_sum(loadings, target_expr), "src")
    target_pc = jnp.take(target_all, local_order, axis=1)
    src_share = 1.0 / jnp.float32(lax.axis_size("tgt"))
    tgt_share = 1.0 / jnp.float32(lax.axis_size("src"))
    src_sq_sum, src_vec, tgt_sq_sum, tgt_vec = lax.psum(
        (
            jnp.sum(source_pc * source_pc) * src_share,
            jnp.sum(source_pc, axis=1) * src_share,
            jnp.sum(target_pc * target_pc) * tgt_share,
            jnp.sum(target_pc, axis=1) * tgt_share,
        ),
        ("src", "tgt"),
    )
    src_mean = src_vec / jnp.float32(total_sources)
    tgt_mean = tgt_vec / jnp.float32(total_targets)
    mean_d2 = (
        src_sq_sum / jnp.float32(total_sources)
        + tgt_sq_sum / jnp.float32(total_targets)
        - 2.0 * jnp.sum(src_mean * tgt_mean)
    )
    spans = 0.5 * (jnp.float32(LEVELS) - time_label.astype(jnp.float32))
    growth = jnp.exp(spans * jnp.clip(score, -2.0, 2.0))
    target_mass = jnp.float32(total_sources) / jnp.float32(total_targets)
    power = 1.0 / 1.1
    stored = build_kernel(source_pc, target_pc, mean_d2)
    scale_v = jnp.ones((columns,), jnp.float32)
    scale_u = jnp.ones((source_pc.shape[1],), jnp.float32)
    for step in range(ITERS):
        row_part = jnp.dot(stored, scale_v, precision=lax.Precision.HIGHEST)
        scale_u = (growth / lax.psum(row_part, "tgt")) ** power
        col_part = jnp.dot(scale_u, stored, precision=lax.Precision.HIGHEST)
        scale_v = (target_mass / lax.psum(col_part, "src")) ** power
    return jnp.float32(total_targets) * scale_u[:, None] * stored * scale_v[None, :]

def proj(left, right):
    return lax.dot_general(left, right, (((1,), (0,)), ((), ())), preferred_element_type=jnp.float32)


def proj_nt(left, right, precision=None):
    return lax.dot_general(
        left, right, (((1,), (1,)), ((), ())), precision=precision, preferred_element_type=jnp.float32
    )


def power_of(x):
    return jnp.exp(jnp.log(x) * (1.0 / 1.1))


def iota(shape, axis):
    return lax.broadcasted_iota(jnp.int32, shape, axis)


def halves(x):
    top = x.astype(jnp.bfloat16).astype(jnp.float32)
    rest = x - top
    middle = rest.astype(jnp.bfloat16).astype(jnp.float32)
    return top, middle, rest - middle


def replicate(row):
    return jnp.transpose(jnp.broadcast_to(row, (128, row.shape[1])))


def fused(
    n, source_hbm, target_hbm, load_ref, panel_hbm, label_hbm, order_hbm, out_ref,
    panel_ref, label_ref, order_ref,
    xs, xt, weights, part_t, recv_x, sum_t, recv_t, part_s, recv_s, all_t, all_s, rows, lookup, perm, moments,
    kern, row_u, col_v,
    load_sem, small_sem, rx_send, rx_recv, rt_send, rt_recv, rs_send, rs_recv, as_send, as_recv, fs_send, fs_recv,
    ax_send, ax_recv, az_send, az_recv, fw_send, fw_recv, it_send, it_recv,
):
    me = lax.axis_index("src")
    core = lax.axis_index("tgt")
    nz = n // 2
    x = lax.rem(me, 2)
    z = me // 2
    beside = 2 * z + 1 - x
    components, genes = load_ref.shape
    width = xt.shape[2]
    half_s = xs.shape[1]
    high = part_t.shape[1]
    n_targets = target_hbm.shape[1]
    n_sources = source_hbm.shape[1]
    own = out_ref.shape[0]
    columns = out_ref.shape[1]
    deep = 8 * n

    def peer(d):
        return lax.rem(me + d, n)

    def along(d):
        return lax.rem(z + d, nz)

    def remote(src, dst, send, recv, s, c):
        return pltpu.make_async_remote_copy(
            src_ref=src, dst_ref=dst, send_sem=send, recv_sem=recv,
            device_id={"src": s, "tgt": c}, device_id_type=pl.DeviceIdType.MESH,
        )

    sends = []

    def go(copy):
        copy.start()
        sends.append(copy)

    turn = [n // 2 + k * sign for k in range(n // 2) for sign in ((1, -1) if k else (1,))]
    line = [nz // 2] + [d for d in range(1, nz) if d != nz // 2] + [0]

    barrier = pltpu.get_barrier_semaphore()
    for d in range(1, n):
        pl.semaphore_signal(
            barrier, inc=1, device_id={"src": peer(d), "tgt": core}, device_id_type=pl.DeviceIdType.MESH
        )
    pl.semaphore_signal(
        barrier, inc=1, device_id={"src": me, "tgt": 1 - core}, device_id_type=pl.DeviceIdType.MESH
    )

    small = []
    my_columns = pl.multiple_of(core * columns, 128)
    for k, (src, dst) in enumerate((
        (panel_hbm, panel_ref), (label_hbm, label_ref),
        (order_hbm.at[:, pl.ds(my_columns, columns)], order_ref),
    )):
        small.append(pltpu.make_async_copy(src, dst, small_sem.at[k]))
        small[-1].start()
    plan = [(d, 2 * along(d) + 1 - x) for d in line] + [(d, 2 * along(d) + x) for d in line]
    load_s = pltpu.make_async_copy(
        source_hbm.at[:, pl.ds(pl.multiple_of(core * half_s, 128), half_s)], xs, load_sem.at[n]
    )
    loads = []
    for k, (d, s) in enumerate(plan):
        if k == nz:
            load_s.start()
        start = pl.multiple_of(core * columns + s * width, 128)
        load = pltpu.make_async_copy(target_hbm.at[:, pl.ds(start, width)], xt.at[k], load_sem.at[k])
        load.start()
        loads.append(load)

    base = jnp.concatenate(
        [load_ref[...].astype(jnp.float32), jnp.zeros((deep - components, genes), jnp.float32)], axis=0
    )
    weights[0] = base.astype(jnp.bfloat16)

    def project(k):
        loads[k].wait()
        return proj(weights[0], xt[k])[:high]

    for k in range(nz):
        zz = along(plan[k][0])
        part_t[k] = project(k)
        if k == 0:
            pl.semaphore_wait(barrier, n)
        go(remote(part_t.at[k], recv_x.at[zz], rx_send.at[k], rx_recv.at[zz], beside, core))

    for copy in small:
        copy.wait()
    hits = (iota((genes, panel_ref.shape[1]), 0) + me * genes == panel_ref[...]).astype(jnp.float32)
    pick = (iota((deep, panel_ref.shape[1]), 0) == components).astype(jnp.bfloat16)
    counts = proj_nt(pick, hits.astype(jnp.bfloat16))
    weights[1] = (weights[0].astype(jnp.float32) + counts).astype(jnp.bfloat16)
    spans = 0.5 * (LEVELS - label_ref[...].astype(jnp.float32))
    place = (iota((own, half_s), 0) + me * own == iota((own, half_s), 1) + core * half_s).astype(jnp.bfloat16)
    placed = proj(jnp.broadcast_to(spans, (16, own)).astype(jnp.bfloat16), place)[0:1]
    load_s.wait()
    source_part = proj(weights[1], xs[...])
    part_s[...] = jnp.where(iota((deep, half_s), 0) == components + 1, placed, source_part)
    recv_s[me] = part_s[pl.ds(pl.multiple_of(me * 8, 8), 8), :]
    for d in turn:
        p = peer(d)
        go(remote(part_s.at[pl.ds(pl.multiple_of(p * 8, 8), 8)], recv_s.at[me], rs_send.at[d], rs_recv.at[me], p, core))

    for k in range(nz, n):
        d, s = plan[k]
        zz = along(d)
        block = project(k)
        remote(recv_x.at[zz], recv_x.at[zz], rx_send.at[k - nz], rx_recv.at[zz], beside, core).wait_recv()
        block = block + recv_x[zz]
        if d:
            sum_t[d] = block
            go(remote(sum_t.at[d], recv_t.at[z], rt_send.at[d], rt_recv.at[z], s, core))
        else:
            recv_t[z] = block

    for d in turn:
        p = peer(d)
        remote(recv_s.at[p], recv_s.at[p], rs_send.at[d], rs_recv.at[p], p, core).wait_recv()
    my_lanes = pl.ds(pl.multiple_of(core * half_s, 128), half_s)
    other_lanes = pl.ds(pl.multiple_of((1 - core) * half_s, 128), half_s)

    def rows_of(s):
        return pl.ds(pl.multiple_of(s * 8, 8), 8)

    total = recv_s[0]
    for s in range(1, n):
        total = total + recv_s[s]
    all_s[rows_of(me), my_lanes] = total
    here = all_s.at[rows_of(me), my_lanes]
    for d in turn:
        go(remote(here, here, as_send.at[d], as_recv.at[me], peer(d), core))
    go(remote(here, here, fs_send.at[0], fs_recv.at[me], me, 1 - core))

    order = order_ref[...]
    block_of = order // width
    lookup[...] = (iota((width, columns), 0) == order - block_of * width).astype(jnp.float32).astype(jnp.bfloat16)
    perm[...] = jnp.zeros_like(perm)
    moments[...] = jnp.zeros_like(moments)

    def place_pair(first, second):
        parts = []
        for index in (first, second):
            block = all_t[index]
            moments[0] += block
            moments[1] += block * block
            parts += halves(block)
        found = proj(jnp.concatenate(parts, axis=0).astype(jnp.bfloat16), lookup[...])
        one = (found[:high] + found[high : 2 * high]) + found[2 * high : 3 * high]
        two = (found[3 * high : 4 * high] + found[4 * high : 5 * high]) + found[5 * high :]
        perm[:high] = jnp.where(block_of == first, one, jnp.where(block_of == second, two, perm[:high]))

    for d in line[:-1]:
        zz = along(d)
        remote(recv_t.at[zz], recv_t.at[zz], rt_send.at[d], rt_recv.at[zz], 2 * zz + x, core).wait_recv()
    mine = recv_t[0]
    for s in range(1, nz):
        mine = mine + recv_t[s]
    slot = core * n + me
    all_t[slot] = mine
    here = all_t.at[slot]
    for d in line[:-1]:
        go(remote(here, here, az_send.at[d], az_recv.at[z], 2 * along(d) + x, core))
    go(remote(here, here, ax_send.at[0], ax_recv.at[z], beside, core))
    go(remote(here, here, fw_send.at[0], fw_recv.at[me], me, 1 - core))

    for d in turn:
        p = peer(d)
        there = all_s.at[rows_of(p), my_lanes]
        remote(there, there, as_send.at[d], as_recv.at[p], p, core).wait_recv()
        go(remote(there, there, fs_send.at[d], fs_recv.at[p], me, 1 - core))

    def nth(k):
        across = k // nz
        zz = lax.rem(z + k, nz)
        return zz, 2 * zz + x + across * (1 - 2 * x)

    def by_line(k):
        zz, s = nth(k)
        there = all_t.at[core * n + s]
        return remote(there, there, az_send.at[k], az_recv.at[zz], s, core)

    def by_x(k):
        zz, s = nth(k)
        there = all_t.at[core * n + s]
        return remote(there, there, ax_send.at[lax.rem(k, nz)], ax_recv.at[zz], beside, core)

    def by_core(k, c):
        zz, s = nth(k)
        there = all_t.at[c * n + s]
        return remote(there, there, fw_send.at[k], fw_recv.at[s], me, 1 - core)

    @pl.loop(1, n + 1)
    def _(k):
        @pl.when(k < nz)
        def _():
            by_line(k).wait_recv()
            by_x(k).start()
            by_core(k, core).start()

        @pl.when((k >= nz) & (k < n))
        def _():
            by_x(k).wait_recv()
            by_core(k, core).start()

        by_core(k - 1, 1 - core).wait_recv()
        zz, s = nth(k - 1)
        place_pair(core * n + s, (1 - core) * n + s)

    for d in range(n):
        p = peer(d)
        there = all_s.at[rows_of(p), other_lanes]
        remote(there, there, fs_send.at[d], fs_recv.at[p], me, 1 - core).wait_recv()
    source = all_s[...]
    growth = jnp.exp(
        source[components + 1 : components + 2]
        * jnp.clip(source[components : components + 1] / jnp.sqrt(jnp.float32(panel_ref.shape[1])), -2.0, 2.0)
    )
    pcs = jnp.where(iota(source.shape, 0) < components, source, 0.0)
    source_sq = jnp.sum(pcs * pcs, axis=0, keepdims=True)
    source_rep = replicate(source_sq)
    turned = jnp.transpose(jnp.concatenate([pcs, jnp.zeros((128 - deep, n_sources), jnp.float32)], axis=0))
    s_top, s_mid, s_low = halves(turned[:, :deep])
    left = jnp.concatenate([s_top, s_mid, s_top, s_mid, s_low, s_top], axis=1).astype(jnp.bfloat16)

    target_sum = jnp.sum(moments[0], axis=1, keepdims=True)
    target_sq = jnp.sum(jnp.sum(moments[1], axis=1, keepdims=True), axis=0, keepdims=True)
    source_sum = jnp.sum(pcs[:high], axis=1, keepdims=True)
    mean = (
        jnp.sum(source_sq, axis=1, keepdims=True) / n_sources
        + target_sq / n_targets
        - 2.0 * jnp.sum((source_sum / n_sources) * (target_sum / n_targets), axis=0, keepdims=True)
    )
    factor = -1.0 / (0.1 * mean)
    tiles = columns // 128

    def lanes(t):
        return slice(t * 128, t * 128 + 128)

    step_rows = 64

    @pl.loop(0, tiles // 2)
    def _(t):
        part = perm[:, pl.ds(pl.multiple_of(t * 256, 256), 256)]
        norm = jnp.sum(part * part, axis=0, keepdims=True)
        t_top, t_mid, t_low = halves(part)
        right = jnp.concatenate([t_top, t_top, t_mid, t_mid, t_top, t_low], axis=0).astype(jnp.bfloat16)
        cross = proj(left, right)
        for h in range(2):
            d2 = source_rep + norm[:, lanes(h)] - 2.0 * cross[:, lanes(h)]
            kern[:, pl.ds(pl.multiple_of(t * 256 + h * 128, 128), 128)] = jnp.exp(d2 * factor)

    def row_sums(scale):
        out = []
        for r in range(0, n_sources, step_rows):
            acc = None
            for t in range(tiles):
                term = kern[r : r + step_rows, lanes(t)]
                if scale:
                    term = term * col_v[:, lanes(t)]
                acc = term if acc is None else acc + term
            out.append(acc)
        return jnp.sum(jnp.transpose(jnp.concatenate(out, axis=0)), axis=0, keepdims=True)

    target_mass = n_sources / n_targets
    for step in range(ITERS):
        rows[step, core] = row_sums(step > 0)
        here = rows.at[step, core]
        go(remote(here, here, it_send.at[step], it_recv.at[step], me, 1 - core))
        there = rows.at[step, 1 - core]
        remote(there, there, it_send.at[step], it_recv.at[step], me, 1 - core).wait_recv()
        row_u[...] = replicate(power_of(growth / (rows[step, 0] + rows[step, 1])))
        for t in range(tiles):
            col_v[:, lanes(t)] = jnp.sum(kern[:, lanes(t)] * row_u[...], axis=0, keepdims=True)
        col_v[...] = power_of(target_mass / col_v[...])
    mine_rows = pl.ds(pl.multiple_of(me * own, 8), own)
    own_u = n_targets * row_u[mine_rows, :]
    for t in range(tiles):
        out_ref[:, lanes(t)] = own_u * kern[mine_rows, lanes(t)] * col_v[:, lanes(t)]
    for copy in sends:
        copy.wait_send()
    for k in range(1, n):
        if k < nz:
            by_x(k).wait_send()
        by_core(k, core).wait_send()


def fused_call(source_expr, target_expr, loadings, panel, time_label, target_order):
    n = lax.axis_size("src")
    genes, components = loadings.shape
    n_sources, n_targets = source_expr.shape[1], target_expr.shape[1]
    own, columns = n_sources // n, n_targets // 2
    width, half_s = columns // n, n_sources // 2
    high = (components + 7) // 8 * 8
    nz = n // 2
    vmem = pltpu.VMEM
    dma = pltpu.SemaphoreType.DMA
    f32, bf16, i32 = jnp.float32, jnp.bfloat16, jnp.int32
    return pl.pallas_call(
        functools.partial(fused, n),
        out_shape=jax.ShapeDtypeStruct((own, columns), f32),
        in_specs=[pl.BlockSpec(memory_space=vmem if k == 2 else pltpu.HBM) for k in range(6)],
        out_specs=pl.BlockSpec(memory_space=vmem),
        scratch_shapes=[
            vmem((1, panel.shape[0]), i32),
            vmem((1, own), i32),
            vmem((1, columns), i32),
            vmem((genes, half_s), bf16),
            vmem((n, genes, width), bf16),
            vmem((2, 8 * n, genes), bf16),
            vmem((nz, high, width), f32),
            vmem((nz, high, width), f32),
            vmem((nz, high, width), f32),
            vmem((nz, high, width), f32),
            vmem((8 * n, half_s), f32),
            vmem((n, 8, half_s), f32),
            vmem((2 * n, high, width), f32),
            vmem((8 * n, n_sources), f32),
            vmem((ITERS, 2, 1, n_sources), f32),
            vmem((width, columns), bf16),
            vmem((8 * n, columns), f32),
            vmem((2, high, width), f32),
            vmem((n_sources, columns), f32),
            vmem((n_sources, 128), f32),
            vmem((1, columns), f32),
            dma((n + 1,)), dma((3,)),
            dma((nz,)), dma((nz,)), dma((nz,)), dma((nz,)),
            dma((n,)), dma((n,)), dma((n,)), dma((n,)), dma((n,)), dma((n,)),
            dma((nz,)), dma((nz,)), dma((nz,)), dma((nz,)),
            dma((n,)), dma((n,)), dma((ITERS,)), dma((ITERS,)),
        ],
        compiler_params=pltpu.CompilerParams(
            collective_id=0, has_side_effects=True, vmem_limit_bytes=56 * 1024 * 1024
        ),
    )(
        source_expr, target_expr, loadings.T,
        panel.reshape(1, -1), time_label.reshape(1, -1), target_order.reshape(1, -1),
    )


def fits(mesh, source_expr, target_expr, loadings, time_label):
    n = mesh.shape["src"]
    components = loadings.shape[1]
    n_sources, n_targets = source_expr.shape[1], target_expr.shape[1]
    return (
        mesh.shape["tgt"] == 2
        and n % 2 == 0
        and components + 2 <= 8 * n
        and 8 * n <= 128
        and n_sources % 256 == 0
        and n_sources * n_targets <= 2 * 1024 * 1024
        and n_targets % (2 * n * 128) == 0
        and loadings.shape[0] % 128 == 0
        and loadings.shape[0] * (n_targets + n_sources) <= 32 * 1024 * 1024
    )


def solution(mesh):
    def per_device(*arrays):
        if fits(mesh, arrays[0], arrays[1], arrays[2], arrays[4]):
            return fused_call(*arrays)
        return local(*arrays)

    return jax.shard_map(
        per_device,
        mesh=mesh,
        in_specs=(
            P("src", "pairs"),
            P("src", "pairs"),
            P("src", None),
            P(),
            P(("pairs", "src")),
            P("pairs"),
        ),
        out_specs=P(("pairs", "src"), "tgt"),
        check_vma=False,
    )
```

```python
import functools

import jax
import jax.numpy as jnp
from jax import lax
from jax.experimental import pallas as pl
from jax.experimental.pallas import tpu as pltpu
from jax.sharding import PartitionSpec as P

LEVELS = 4
ITERS = 3


def gene_sum(left, right):
    return lax.dot_general(
        left, right, (((0,), (0,)), ((), ())), preferred_element_type=jnp.float32
    )


def build_kernel(source_pc, target_pc, mean_d2):
    src_sq = jnp.sum(source_pc * source_pc, axis=0)
    tgt_sq = jnp.sum(target_pc * target_pc, axis=0)
    cross = lax.dot_general(
        source_pc, target_pc, (((0,), (0,)), ((), ())), precision=lax.Precision.HIGHEST
    )
    d2 = src_sq[:, None] + tgt_sq[None, :] - 2.0 * cross
    return jnp.exp(-(d2 / mean_d2) / 0.1)


def local(source_expr, target_expr, loadings, panel, time_label, target_order):
    genes = source_expr.shape[0]
    first_gene = lax.axis_index("src") * genes
    gene_ids = first_gene + lax.broadcasted_iota(jnp.int32, (genes, panel.shape[0]), 0)
    counts = jnp.sum((gene_ids == panel[None, :]).astype(jnp.float32), axis=1).astype(jnp.bfloat16)
    source_pc = lax.psum_scatter(
        gene_sum(loadings, source_expr), "src", scatter_dimension=1, tiled=True
    )
    score_part = jnp.dot(counts[None, :], source_expr, preferred_element_type=jnp.float32)
    score_raw = lax.psum_scatter(score_part, "src", scatter_dimension=1, tiled=True)[0]
    score = score_raw / jnp.sqrt(jnp.float32(panel.shape[0]))
    total_targets = target_expr.shape[1]
    total_sources = source_expr.shape[1]
    columns = total_targets // lax.axis_size("tgt")
    local_order = lax.dynamic_slice_in_dim(target_order, lax.axis_index("tgt") * columns, columns)
    target_all = lax.psum(gene_sum(loadings, target_expr), "src")
    target_pc = jnp.take(target_all, local_order, axis=1)
    src_share = 1.0 / jnp.float32(lax.axis_size("tgt"))
    tgt_share = 1.0 / jnp.float32(lax.axis_size("src"))
    src_sq_sum, src_vec, tgt_sq_sum, tgt_vec = lax.psum(
        (
            jnp.sum(source_pc * source_pc) * src_share,
            jnp.sum(source_pc, axis=1) * src_share,
            jnp.sum(target_pc * target_pc) * tgt_share,
            jnp.sum(target_pc, axis=1) * tgt_share,
        ),
        ("src", "tgt"),
    )
    src_mean = src_vec / jnp.float32(total_sources)
    tgt_mean = tgt_vec / jnp.float32(total_targets)
    mean_d2 = (
        src_sq_sum / jnp.float32(total_sources)
        + tgt_sq_sum / jnp.float32(total_targets)
        - 2.0 * jnp.sum(src_mean * tgt_mean)
    )
    spans = 0.5 * (jnp.float32(LEVELS) - time_label.astype(jnp.float32))
    growth = jnp.exp(spans * jnp.clip(score, -2.0, 2.0))
    target_mass = jnp.float32(total_sources) / jnp.float32(total_targets)
    power = 1.0 / 1.1
    stored = build_kernel(source_pc, target_pc, mean_d2)
    scale_v = jnp.ones((columns,), jnp.float32)
    scale_u = jnp.ones((source_pc.shape[1],), jnp.float32)
    for step in range(ITERS):
        row_part = jnp.dot(stored, scale_v, precision=lax.Precision.HIGHEST)
        scale_u = (growth / lax.psum(row_part, "tgt")) ** power
        col_part = jnp.dot(scale_u, stored, precision=lax.Precision.HIGHEST)
        scale_v = (target_mass / lax.psum(col_part, "src")) ** power
    return jnp.float32(total_targets) * scale_u[:, None] * stored * scale_v[None, :]

def proj(left, right):
    return lax.dot_general(left, right, (((1,), (0,)), ((), ())), preferred_element_type=jnp.float32)


def proj_nt(left, right, precision=None):
    return lax.dot_general(
        left, right, (((1,), (1,)), ((), ())), precision=precision, preferred_element_type=jnp.float32
    )


def power_of(x):
    return jnp.exp(jnp.log(x) * (1.0 / 1.1))


def iota(shape, axis):
    return lax.broadcasted_iota(jnp.int32, shape, axis)


def halves(x):
    top = x.astype(jnp.bfloat16).astype(jnp.float32)
    rest = x - top
    middle = rest.astype(jnp.bfloat16).astype(jnp.float32)
    return top, middle, rest - middle


def replicate(row):
    return jnp.transpose(jnp.broadcast_to(row, (128, row.shape[1])))


def fused(
    n, source_hbm, target_hbm, load_ref, panel_hbm, label_hbm, order_hbm, out_ref,
    panel_ref, label_ref, order_ref,
    xs, xt, weights, part_t, recv_x, sum_t, recv_t, part_s, recv_s, all_t, all_s, rows, lookup, perm, moments,
    kern, row_u, col_v,
    load_sem, small_sem, rx_send, rx_recv, rt_send, rt_recv, rs_send, rs_recv, as_send, as_recv, fs_send, fs_recv,
    ax_send, ax_recv, az_send, az_recv, fw_send, fw_recv, it_send, it_recv,
):
    me = lax.axis_index("src")
    core = lax.axis_index("tgt")
    nz = n // 2
    x = lax.rem(me, 2)
    z = me // 2
    beside = 2 * z + 1 - x
    components, genes = load_ref.shape
    width = xt.shape[2]
    half_s = xs.shape[1]
    high = part_t.shape[1]
    n_targets = target_hbm.shape[1]
    n_sources = source_hbm.shape[1]
    own = out_ref.shape[0]
    columns = out_ref.shape[1]
    deep = 8 * n

    def peer(d):
        return lax.rem(me + d, n)

    def along(d):
        return lax.rem(z + d, nz)

    def remote(src, dst, send, recv, s, c):
        return pltpu.make_async_remote_copy(
            src_ref=src, dst_ref=dst, send_sem=send, recv_sem=recv,
            device_id={"src": s, "tgt": c}, device_id_type=pl.DeviceIdType.MESH,
        )

    sends = []

    def go(copy):
        copy.start()
        sends.append(copy)

    turn = [n // 2 + k * sign for k in range(n // 2) for sign in ((1, -1) if k else (1,))]
    line = list(range(nz))[::-1]

    barrier = pltpu.get_barrier_semaphore()
    for d in range(1, n):
        pl.semaphore_signal(
            barrier, inc=1, device_id={"src": peer(d), "tgt": core}, device_id_type=pl.DeviceIdType.MESH
        )
    pl.semaphore_signal(
        barrier, inc=1, device_id={"src": me, "tgt": 1 - core}, device_id_type=pl.DeviceIdType.MESH
    )

    small = []
    my_columns = pl.multiple_of(core * columns, 128)
    for k, (src, dst) in enumerate((
        (panel_hbm, panel_ref), (label_hbm, label_ref),
        (order_hbm.at[:, pl.ds(my_columns, columns)], order_ref),
    )):
        small.append(pltpu.make_async_copy(src, dst, small_sem.at[k]))
        small[-1].start()
    plan = [(d, 2 * along(d) + 1 - x) for d in line] + [(d, 2 * along(d) + x) for d in line]
    load_s = pltpu.make_async_copy(
        source_hbm.at[:, pl.ds(pl.multiple_of(core * half_s, 128), half_s)], xs, load_sem.at[n]
    )
    for k, (d, s) in enumerate(plan):
        if k == nz:
            load_s.start()
        start = pl.multiple_of(core * columns + s * width, 128)
        load = pltpu.make_async_copy(target_hbm.at[:, pl.ds(start, width)], xt.at[k], load_sem.at[k])
        load.start()

    base = jnp.concatenate(
        [load_ref[...].astype(jnp.float32), jnp.zeros((deep - components, genes), jnp.float32)], axis=0
    )
    weights[0] = base.astype(jnp.bfloat16)

    def project(k):
        pltpu.make_async_copy(target_hbm.at[:, pl.ds(0, width)], xt.at[k], load_sem.at[k]).wait()
        return proj(weights[0], xt[k])[:high]

    def x_step(k):
        zz = along(nz - 1 - k)
        return remote(part_t.at[k], recv_x.at[zz], rx_send.at[k], rx_recv.at[zz], beside, core)

    def z_step(d):
        return remote(sum_t.at[d], recv_t.at[z], rt_send.at[d], rt_recv.at[z], 2 * along(d) + x, core)

    pl.semaphore_wait(barrier, n)

    @pl.loop(0, nz)
    def _(k):
        part_t[k] = project(k)
        x_step(k).start()

    for copy in small:
        copy.wait()
    hits = (iota((genes, panel_ref.shape[1]), 0) + me * genes == panel_ref[...]).astype(jnp.float32)
    pick = (iota((deep, panel_ref.shape[1]), 0) == components).astype(jnp.bfloat16)
    counts = proj_nt(pick, hits.astype(jnp.bfloat16))
    weights[1] = (weights[0].astype(jnp.float32) + counts).astype(jnp.bfloat16)
    spans = 0.5 * (LEVELS - label_ref[...].astype(jnp.float32))
    place = (iota((own, half_s), 0) + me * own == iota((own, half_s), 1) + core * half_s).astype(jnp.bfloat16)
    placed = proj(jnp.broadcast_to(spans, (16, own)).astype(jnp.bfloat16), place)[0:1]
    load_s.wait()
    source_part = proj(weights[1], xs[...])
    part_s[...] = jnp.where(iota((deep, half_s), 0) == components + 1, placed, source_part)
    recv_s[me] = part_s[pl.ds(pl.multiple_of(me * 8, 8), 8), :]
    for d in turn:
        p = peer(d)
        go(remote(part_s.at[pl.ds(pl.multiple_of(p * 8, 8), 8)], recv_s.at[me], rs_send.at[d], rs_recv.at[me], p, core))

    @pl.loop(0, nz)
    def _(k):
        d = nz - 1 - k
        zz = along(d)
        block = project(nz + k)
        remote(recv_x.at[zz], recv_x.at[zz], rx_send.at[k], rx_recv.at[zz], beside, core).wait_recv()
        block = block + recv_x[zz]

        @pl.when(d > 0)
        def _():
            sum_t[d] = block
            z_step(d).start()

        @pl.when(d == 0)
        def _():
            recv_t[z] = block

    for d in turn:
        p = peer(d)
        remote(recv_s.at[p], recv_s.at[p], rs_send.at[d], rs_recv.at[p], p, core).wait_recv()
    my_lanes = pl.ds(pl.multiple_of(core * half_s, 128), half_s)
    other_lanes = pl.ds(pl.multiple_of((1 - core) * half_s, 128), half_s)

    def rows_of(s):
        return pl.ds(pl.multiple_of(s * 8, 8), 8)

    total = recv_s[0]
    for s in range(1, n):
        total = total + recv_s[s]
    all_s[rows_of(me), my_lanes] = total
    here = all_s.at[rows_of(me), my_lanes]
    for d in turn:
        go(remote(here, here, as_send.at[d], as_recv.at[me], peer(d), core))
    go(remote(here, here, fs_send.at[0], fs_recv.at[me], me, 1 - core))

    order = order_ref[...]
    block_of = order // width
    lookup[...] = (iota((width, columns), 0) == order - block_of * width).astype(jnp.float32).astype(jnp.bfloat16)
    perm[...] = jnp.zeros_like(perm)
    moments[...] = jnp.zeros_like(moments)

    def place_pair(first, second):
        parts = []
        for index in (first, second):
            block = all_t[index]
            moments[0] += block
            moments[1] += block * block
            parts += halves(block)
        found = proj(jnp.concatenate(parts, axis=0).astype(jnp.bfloat16), lookup[...])
        one = (found[:high] + found[high : 2 * high]) + found[2 * high : 3 * high]
        two = (found[3 * high : 4 * high] + found[4 * high : 5 * high]) + found[5 * high :]
        perm[:high] = jnp.where(block_of == first, one, jnp.where(block_of == second, two, perm[:high]))

    for d in line[:-1]:
        zz = along(d)
        remote(recv_t.at[zz], recv_t.at[zz], rt_send.at[d], rt_recv.at[zz], 2 * zz + x, core).wait_recv()
    mine = recv_t[0]
    for s in range(1, nz):
        mine = mine + recv_t[s]
    slot = core * n + me
    all_t[slot] = mine
    here = all_t.at[slot]
    for d in line[:-1]:
        go(remote(here, here, az_send.at[d], az_recv.at[z], 2 * along(d) + x, core))
    go(remote(here, here, ax_send.at[0], ax_recv.at[z], beside, core))
    go(remote(here, here, fw_send.at[0], fw_recv.at[me], me, 1 - core))

    for d in turn:
        p = peer(d)
        there = all_s.at[rows_of(p), my_lanes]
        remote(there, there, as_send.at[d], as_recv.at[p], p, core).wait_recv()
        go(remote(there, there, fs_send.at[d], fs_recv.at[p], me, 1 - core))

    def nth(k):
        across = k // nz
        zz = lax.rem(z + k, nz)
        return zz, 2 * zz + x + across * (1 - 2 * x)

    def by_line(k):
        zz, s = nth(k)
        there = all_t.at[core * n + s]
        return remote(there, there, az_send.at[k], az_recv.at[zz], s, core)

    def by_x(k):
        zz, s = nth(k)
        there = all_t.at[core * n + s]
        return remote(there, there, ax_send.at[lax.rem(k, nz)], ax_recv.at[zz], beside, core)

    def by_core(k, c):
        zz, s = nth(k)
        there = all_t.at[c * n + s]
        return remote(there, there, fw_send.at[k], fw_recv.at[s], me, 1 - core)

    @pl.loop(1, n + 1)
    def _(k):
        @pl.when(k < nz)
        def _():
            by_line(k).wait_recv()
            by_x(k).start()
            by_core(k, core).start()

        @pl.when((k >= nz) & (k < n))
        def _():
            by_x(k).wait_recv()
            by_core(k, core).start()

        by_core(k - 1, 1 - core).wait_recv()
        zz, s = nth(k - 1)
        place_pair(core * n + s, (1 - core) * n + s)

    for d in range(n):
        p = peer(d)
        there = all_s.at[rows_of(p), other_lanes]
        remote(there, there, fs_send.at[d], fs_recv.at[p], me, 1 - core).wait_recv()
    source = all_s[...]
    growth = jnp.exp(
        source[components + 1 : components + 2]
        * jnp.clip(source[components : components + 1] / jnp.sqrt(jnp.float32(panel_ref.shape[1])), -2.0, 2.0)
    )
    pcs = jnp.where(iota(source.shape, 0) < components, source, 0.0)
    source_sq = jnp.sum(pcs * pcs, axis=0, keepdims=True)
    source_rep = replicate(source_sq)
    turned = jnp.transpose(jnp.concatenate([pcs, jnp.zeros((128 - deep, n_sources), jnp.float32)], axis=0))
    s_top, s_mid, s_low = halves(turned[:, :deep])
    left = jnp.concatenate([s_top, s_mid, s_top, s_mid, s_low, s_top], axis=1).astype(jnp.bfloat16)

    target_sum = jnp.sum(moments[0], axis=1, keepdims=True)
    target_sq = jnp.sum(jnp.sum(moments[1], axis=1, keepdims=True), axis=0, keepdims=True)
    source_sum = jnp.sum(pcs[:high], axis=1, keepdims=True)
    mean = (
        jnp.sum(source_sq, axis=1, keepdims=True) / n_sources
        + target_sq / n_targets
        - 2.0 * jnp.sum((source_sum / n_sources) * (target_sum / n_targets), axis=0, keepdims=True)
    )
    factor = -1.0 / (0.1 * mean)
    tiles = columns // 128

    def lanes(t):
        return slice(t * 128, t * 128 + 128)

    step_rows = 64

    @pl.loop(0, tiles // 2)
    def _(t):
        part = perm[:, pl.ds(pl.multiple_of(t * 256, 256), 256)]
        norm = jnp.sum(part * part, axis=0, keepdims=True)
        t_top, t_mid, t_low = halves(part)
        right = jnp.concatenate([t_top, t_top, t_mid, t_mid, t_top, t_low], axis=0).astype(jnp.bfloat16)
        cross = proj(left, right)
        for h in range(2):
            d2 = source_rep + norm[:, lanes(h)] - 2.0 * cross[:, lanes(h)]
            kern[:, pl.ds(pl.multiple_of(t * 256 + h * 128, 128), 128)] = jnp.exp(d2 * factor)

    def row_sums(scale):
        out = []
        for r in range(0, n_sources, step_rows):
            acc = None
            for t in range(tiles):
                term = kern[r : r + step_rows, lanes(t)]
                if scale:
                    term = term * col_v[:, lanes(t)]
                acc = term if acc is None else acc + term
            out.append(acc)
        return jnp.sum(jnp.transpose(jnp.concatenate(out, axis=0)), axis=0, keepdims=True)

    target_mass = n_sources / n_targets
    for step in range(ITERS):
        rows[step, core] = row_sums(step > 0)
        here = rows.at[step, core]
        go(remote(here, here, it_send.at[step], it_recv.at[step], me, 1 - core))
        there = rows.at[step, 1 - core]
        remote(there, there, it_send.at[step], it_recv.at[step], me, 1 - core).wait_recv()
        row_u[...] = replicate(power_of(growth / (rows[step, 0] + rows[step, 1])))
        for t in range(tiles):
            col_v[:, lanes(t)] = jnp.sum(kern[:, lanes(t)] * row_u[...], axis=0, keepdims=True)
        col_v[...] = power_of(target_mass / col_v[...])
    mine_rows = pl.ds(pl.multiple_of(me * own, 8), own)
    own_u = n_targets * row_u[mine_rows, :]
    for t in range(tiles):
        out_ref[:, lanes(t)] = own_u * kern[mine_rows, lanes(t)] * col_v[:, lanes(t)]
    for copy in sends:
        copy.wait_send()
    for k in range(nz):
        x_step(k).wait_send()
        if k:
            z_step(k).wait_send()
    for k in range(1, n):
        if k < nz:
            by_x(k).wait_send()
        by_core(k, core).wait_send()


def fused_call(source_expr, target_expr, loadings, panel, time_label, target_order):
    n = lax.axis_size("src")
    genes, components = loadings.shape
    n_sources, n_targets = source_expr.shape[1], target_expr.shape[1]
    own, columns = n_sources // n, n_targets // 2
    width, half_s = columns // n, n_sources // 2
    high = (components + 7) // 8 * 8
    nz = n // 2
    vmem = pltpu.VMEM
    dma = pltpu.SemaphoreType.DMA
    f32, bf16, i32 = jnp.float32, jnp.bfloat16, jnp.int32
    return pl.pallas_call(
        functools.partial(fused, n),
        out_shape=jax.ShapeDtypeStruct((own, columns), f32),
        in_specs=[pl.BlockSpec(memory_space=vmem if k == 2 else pltpu.HBM) for k in range(6)],
        out_specs=pl.BlockSpec(memory_space=vmem),
        scratch_shapes=[
            vmem((1, panel.shape[0]), i32),
            vmem((1, own), i32),
            vmem((1, columns), i32),
            vmem((genes, half_s), bf16),
            vmem((n, genes, width), bf16),
            vmem((2, 8 * n, genes), bf16),
            vmem((nz, high, width), f32),
            vmem((nz, high, width), f32),
            vmem((nz, high, width), f32),
            vmem((nz, high, width), f32),
            vmem((8 * n, half_s), f32),
            vmem((n, 8, half_s), f32),
            vmem((2 * n, high, width), f32),
            vmem((8 * n, n_sources), f32),
            vmem((ITERS, 2, 1, n_sources), f32),
            vmem((width, columns), bf16),
            vmem((8 * n, columns), f32),
            vmem((2, high, width), f32),
            vmem((n_sources, columns), f32),
            vmem((n_sources, 128), f32),
            vmem((1, columns), f32),
            dma((n + 1,)), dma((3,)),
            dma((nz,)), dma((nz,)), dma((nz,)), dma((nz,)),
            dma((n,)), dma((n,)), dma((n,)), dma((n,)), dma((n,)), dma((n,)),
            dma((nz,)), dma((nz,)), dma((nz,)), dma((nz,)),
            dma((n,)), dma((n,)), dma((ITERS,)), dma((ITERS,)),
        ],
        compiler_params=pltpu.CompilerParams(
            collective_id=0, has_side_effects=True, vmem_limit_bytes=56 * 1024 * 1024
        ),
    )(
        source_expr, target_expr, loadings.T,
        panel.reshape(1, -1), time_label.reshape(1, -1), target_order.reshape(1, -1),
    )


def fits(mesh, source_expr, target_expr, loadings, time_label):
    n = mesh.shape["src"]
    components = loadings.shape[1]
    n_sources, n_targets = source_expr.shape[1], target_expr.shape[1]
    return (
        mesh.shape["tgt"] == 2
        and n % 2 == 0
        and components + 2 <= 8 * n
        and 8 * n <= 128
        and n_sources % 256 == 0
        and n_sources * n_targets <= 2 * 1024 * 1024
        and n_targets % (2 * n * 128) == 0
        and loadings.shape[0] % 128 == 0
        and loadings.shape[0] * (n_targets + n_sources) <= 32 * 1024 * 1024
    )


def solution(mesh):
    def per_device(*arrays):
        if fits(mesh, arrays[0], arrays[1], arrays[2], arrays[4]):
            return fused_call(*arrays)
        return local(*arrays)

    return jax.shard_map(
        per_device,
        mesh=mesh,
        in_specs=(
            P("src", "pairs"),
            P("src", "pairs"),
            P("src", None),
            P(),
            P(("pairs", "src")),
            P("pairs"),
        ),
        out_specs=P(("pairs", "src"), "tgt"),
        check_vma=False,
    )
```
